256 devices in a mesh: row: 32 (over y, z_lo, x), col: 8 (over z_hi, core).
Axes of the slice: x: 4, y: 4, z: 8 (z_hi: 4, z_lo: 2; z = z_hi * 2 + z_lo), core: 2. Of those that a mesh axis runs over, the one named last changes fastest.
Arguments:
- window_factors: bfloat16 [4, 512, 1536], P(None, 'col', 'row'), may hold values from -6 to 6
- factors: bfloat16 [512, 512, 1536], P('col', 'row'), may hold values from -0.15625 to 0.15625
- amplitudes: bfloat16 [512, 512, 512], P(None, 'row', 'col'), may hold values from -0.01171875 to 0.01171875
Outputs:
- ladder: float32 [512, 4, 512], P('col', None, 'row')
The draws below stay inside these ranges and needn't reach their ends.
All inputs are finite; a program needn't handle non-finite values.
Results may differ from the reference program's by a relative error of at most 0.0029.
Values may be sent and summed in bfloat16 or wider, within the bound.
No kernel may reach another device: no remote copies, remote signals or barrier semaphores. Data moves between devices by JAX's collectives and lax.ppermute only.
A program may use at most 64 MiB of HBM per device.

```python
import jax
import jax.numpy as jnp
from jax import lax

NV = 512
NAUX = 1536
AW = 4
PAIRS = 512


def levels(rng, shape, split, smallest, high):
    gain = 1.0
    for position, shards_of in split:
        draws = jax.random.uniform(jax.random.fold_in(jax.random.fold_in(rng, 6), position), (shards_of,), jnp.float32, smallest / len(split), high / len(split))
        gain = gain * jnp.repeat(jnp.exp(draws), shape[position] // shards_of).reshape((-1,) + (1,) * (len(shape) - 1 - position))
    return gain


def centred(own_key, shape, spread, most, pieces=(), dtype=jnp.bfloat16):
    level = levels(own_key, shape, pieces, -0.22, 0.18) if pieces else 1.0
    values = jax.random.normal(own_key, shape, jnp.float32) * spread * level
    return jnp.minimum(jnp.maximum(values, -most), most).astype(dtype)


def setup_inputs(seed: int = 0) -> dict:
    streams_of = jax.random.split(jax.random.key(seed), 4)
    return {
        "window_factors": centred(streams_of[0], (AW, NV, NAUX), 1.0, 6.0, ((1, 8), (2, 32))),
        "factors": centred(streams_of[1], (NV, NV, NAUX), NAUX ** -0.5, 0.15625, ((0, 8), (1, 32))),
        "amplitudes": centred(streams_of[2], (PAIRS, NV, NV), (NV * NV) ** -0.5, 0.01171875, ((1, 32), (2, 8))),
    }


def reference(window_factors, factors, amplitudes):
    factor_rows = factors.reshape(NV * NV, NAUX)
    flat_amps = amplitudes.reshape(PAIRS, NV * NV)

    def one_orbital(orbital_block):
        slab = lax.dot_general(orbital_block, factor_rows, (((1,), (1,)), ((), ())), preferred_element_type=jnp.float32)
        slab = slab.astype(jnp.bfloat16).reshape(NV * NV, NV)
        return jnp.dot(flat_amps, slab, preferred_element_type=jnp.float32)

    ladder = lax.map(one_orbital, window_factors)
    return jnp.transpose(ladder, (1, 0, 2))
```

```python
import jax
import jax.numpy as jnp
from jax import lax
from jax.experimental import pallas as pl
from jax.experimental.pallas import tpu as pltpu
from jax.sharding import PartitionSpec as P

BF16 = jnp.bfloat16
F32 = jnp.float32


def dot(left, right):
    return lax.dot_general(left, right, (((1,), (0,)), ((), ())), preferred_element_type=F32)


def regroup_kernel(amps_ref, out_ref):
    rows, step = amps_ref.shape[0], out_ref.shape[0]
    c_count = 16
    d_count = rows // c_count
    first = pl.program_id(0) * step
    dest = lax.broadcasted_iota(jnp.int32, (step, rows), 0) + first
    src = lax.broadcasted_iota(jnp.int32, (step, rows), 1)
    wanted = (dest % c_count) * d_count + dest // c_count
    select = jnp.where(src == wanted, 1.0, 0.0).astype(BF16)
    out_ref[...] = dot(select, amps_ref[...]).astype(BF16)


def regroup(amps):
    rows, pairs = amps.shape
    step = 256
    return pl.pallas_call(
        regroup_kernel,
        out_shape=jax.ShapeDtypeStruct((rows, pairs), BF16),
        grid=(rows // step,),
        in_specs=[pl.BlockSpec((rows, pairs), lambda g: (0, 0))],
        out_specs=pl.BlockSpec((step, pairs), lambda g: (g, 0)),
        name="regroup_amplitudes",
    )(amps)


def ladder_kernel(own_f, other_f, own_t, other_t, w_ref, out_ref, total):
    g = pl.program_id(0)
    last = pl.num_programs(0) - 1
    half = pl.num_programs(0) // 2

    @pl.when(g == 0)
    def _():
        total[...] = jnp.zeros_like(total)

    def step(f_ref, t_ref):
        factors = f_ref[...].reshape(512, 1536)
        amps = t_ref[...].reshape(512, 512)
        for a in range(2):
            window = w_ref[:, a].reshape(1536, 512)
            integrals = dot(factors, window).astype(BF16)
            total[a] += dot(integrals, amps)

    @pl.when(g < half)
    def _():
        step(own_f, own_t)

    @pl.when(g >= half)
    def _():
        step(other_f, other_t)

    @pl.when(g == last)
    def _():
        for a in range(2):
            out_ref[:, a] = total[a].reshape(32, 16, 512).astype(BF16)


def ladder_part(own_f, other_f, own_t, other_t, window):
    def early(g):
        return (0, jnp.minimum(g, 1), 0, 0)

    def late(g):
        return (0, jnp.maximum(g - 2, 0), 0, 0)

    return pl.pallas_call(
        ladder_kernel,
        out_shape=jax.ShapeDtypeStruct((32, 2, 16, 512), BF16),
        grid=(4,),
        in_specs=[
            pl.BlockSpec((32, 1, 16, 1536), early),
            pl.BlockSpec((32, 1, 16, 1536), late),
            pl.BlockSpec((32, 1, 16, 512), early),
            pl.BlockSpec((32, 1, 16, 512), late),
            pl.BlockSpec((32, 2, 48, 512), lambda g: (0, 0, 0, 0)),
        ],
        out_specs=pl.BlockSpec((32, 2, 16, 512), lambda g: (0, 0, 0, 0)),
        scratch_shapes=[pltpu.VMEM((2, 512, 512), F32)],
        compiler_params=pltpu.CompilerParams(vmem_limit_bytes=48 * 1024 * 1024),
        cost_estimate=pl.CostEstimate(flops=8_600_000_000, bytes_accessed=13_000_000, transcendentals=0),
        name="ladder_part",
    )(own_f, other_f, own_t, other_t, window)


def sum_kernel(parts_ref, out_ref):
    out_ref[...] = jnp.sum(parts_ref[...].astype(F32), axis=0)


def sum_parts(parts):
    return pl.pallas_call(
        sum_kernel,
        out_shape=jax.ShapeDtypeStruct(parts.shape[1:], F32),
        name="sum_parts",
    )(parts)


def exchange(x, axis):
    return lax.all_to_all(x, axis, split_axis=0, concat_axis=0, tiled=True)


SWAP = [(q, q ^ 1) for q in range(8)]


def per_device(window_factors, factors, amplitudes):
    core = lax.axis_index("col") & 1
    window = jnp.transpose(window_factors, (0, 2, 1))
    window = lax.all_gather(window, "col", axis=0, tiled=False)
    window = lax.dynamic_slice_in_dim(window, core * 2, 2, axis=1)
    window = jnp.transpose(window, (1, 2, 0, 3)).reshape(2, 48, 512)
    window = exchange(jnp.broadcast_to(window[None], (32, 2, 48, 512)), "row")

    amps = jnp.transpose(amplitudes, (1, 2, 0)).reshape(1024, 512)
    own_t = exchange(regroup(amps).reshape(32, 2, 16, 512), "row")
    own_f = exchange(factors.reshape(32, 2, 16, 1536), "row")
    other_t = lax.ppermute(own_t, "col", SWAP)
    other_f = lax.ppermute(own_f, "col", SWAP)

    part = ladder_part(own_f, other_f, own_t, other_t, window)
    part = sum_parts(exchange(part, "row"))
    part = jnp.transpose(part.reshape(2, 16, 8, 64), (2, 0, 1, 3))
    part = exchange(part, "col")
    out = jnp.sum(part.reshape(4, 4, 16, 64), axis=0)
    return jnp.transpose(out, (2, 0, 1))


def solution(mesh):
    return jax.shard_map(
        per_device,
        mesh=mesh,
        in_specs=(P(None, "col", "row"), P("col", "row", None), P(None, "row", "col")),
        out_specs=P("col", None, "row"),
        check_vma=False,
    )
```

```python
import jax
import jax.numpy as jnp
from jax import lax
from jax.experimental import pallas as pl
from jax.experimental.pallas import tpu as pltpu
from jax.sharding import Mesh
from jax.sharding import PartitionSpec as P

BF16 = jnp.bfloat16
F32 = jnp.float32
PLANE = ("y", "x")
MIB = 1024 * 1024


def dot(left, right):
    return lax.dot_general(left, right, (((1,), (0,)), ((), ())), preferred_element_type=F32)


def regroup_kernel(amps_ref, out_ref):
    rows, step = amps_ref.shape[0], out_ref.shape[0]
    c_count = 16
    d_count = rows // c_count
    first = pl.program_id(0) * step
    dest = lax.broadcasted_iota(jnp.int32, (step, rows), 0) + first
    src = lax.broadcasted_iota(jnp.int32, (step, rows), 1)
    wanted = (dest % c_count) * d_count + dest // c_count
    select = jnp.where(src == wanted, 1.0, 0.0).astype(BF16)
    out_ref[...] = dot(select, amps_ref[...]).astype(BF16)


def regroup(amps):
    rows, pairs = amps.shape
    step = 256
    return pl.pallas_call(
        regroup_kernel,
        out_shape=jax.ShapeDtypeStruct((rows, pairs), BF16),
        grid=(rows // step,),
        in_specs=[pl.BlockSpec((rows, pairs), lambda g: (0, 0))],
        out_specs=pl.BlockSpec((step, pairs), lambda g: (g, 0)),
        name="regroup_amplitudes",
    )(amps)


def ladder_kernel(f_ref, own_t, far_t, own_w, far_w, *rest):
    start, (out_ref, window, amps, total) = rest[:-4], rest[-4:]
    g = pl.program_id(0)
    zl = lax.axis_index("zl")

    @pl.when(g == 0)
    def _():
        for y in range(4):
            for ref, side in ((own_w, zl), (far_w, 1 - zl)):
                at = pl.multiple_of((2 * y + side) * 192, 192)
                for a in range(2):
                    window[a, pl.ds(at, 192)] = ref[4 * y : 4 * y + 4, a].reshape(192, 512)
        if start:
            total[...] = start[0][...]
        else:
            total[...] = jnp.zeros_like(total)

    for y in range(4):
        for ref, side in ((own_t, zl), (far_t, 1 - zl)):
            at = pl.multiple_of((2 * y + side) * 64, 64)
            for d in range(2):
                amps[d, pl.ds(at, 64)] = ref[4 * y : 4 * y + 4, d].reshape(64, 512)
    factors = f_ref[...].reshape(512, 1536)
    for a in range(2):
        integrals = dot(factors, window[a]).astype(BF16).reshape(16, 2, 16, 512)
        for d in range(2):
            total[a] += dot(integrals[:, d].reshape(256, 512), amps[d])

    @pl.when(g == pl.num_programs(0) - 1)
    def _():
        if start:
            for a in range(2):
                out_ref[:, a] = total[a].reshape(16, 16, 512).astype(BF16)
        else:
            out_ref[...] = total[...]


def ladder_part(factors, own_t, far_t, own_w, far_w, *start):
    def pair(g):
        return (0, g, 0, 0)

    def whole(g):
        return (0, 0, 0, 0)

    out_shape = (16, 2, 16, 512) if start else (2, 256, 512)
    return pl.pallas_call(
        ladder_kernel,
        out_shape=jax.ShapeDtypeStruct(out_shape, BF16 if start else F32),
        grid=(2,),
        in_specs=[
            pl.BlockSpec((16, 2, 16, 1536), pair),
            pl.BlockSpec((16, 2, 16, 512), pair),
            pl.BlockSpec((16, 2, 16, 512), pair),
            pl.BlockSpec((16, 2, 48, 512), whole),
            pl.BlockSpec((16, 2, 48, 512), whole),
        ]
        + [pl.BlockSpec((2, 256, 512), lambda g: (0, 0, 0)) for _ in start],
        out_specs=pl.BlockSpec(out_shape, lambda g: (0,) * len(out_shape)),
        scratch_shapes=[
            pltpu.VMEM((2, 1536, 512), BF16),
            pltpu.VMEM((2, 512, 512), BF16),
            pltpu.VMEM((2, 256, 512), F32),
        ],
        compiler_params=pltpu.CompilerParams(vmem_limit_bytes=40 * MIB),
        cost_estimate=pl.CostEstimate(flops=43_000_000_000, bytes_accessed=9_000_000, transcendentals=0),
        name="ladder_part",
    )(factors, own_t, far_t, own_w, far_w, *start)


def sum_kernel(parts_ref, out_ref):
    out_ref[...] = jnp.sum(parts_ref[...].astype(F32), axis=0)


def sum_parts(parts):
    return pl.pallas_call(
        sum_kernel,
        out_shape=jax.ShapeDtypeStruct(parts.shape[1:], F32),
        name="sum_parts",
    )(parts)


def exchange(x, axis):
    return lax.all_to_all(x, axis, split_axis=0, concat_axis=0, tiled=True)


def other(x, axis):
    return lax.ppermute(x, axis, [(0, 1), (1, 0)])


def per_device(window_factors, factors, amplitudes):
    core = lax.axis_index("core")
    amps = jnp.transpose(amplitudes, (1, 2, 0)).reshape(1024, 512)
    own_t = exchange(regroup(amps).reshape(16, 4, 16, 512), PLANE)
    far_t = other(own_t, "zl")

    window = jnp.transpose(window_factors, (0, 2, 1))
    window = lax.all_gather(window, ("zh", "core"), axis=0, tiled=False)
    window = lax.dynamic_slice_in_dim(window, core * 2, 2, axis=1)
    window = jnp.transpose(window, (1, 2, 0, 3)).reshape(2, 48, 512)
    window, _ = lax.optimization_barrier((window, own_t))
    own_w = exchange(jnp.broadcast_to(window[None], (16, 2, 48, 512)), PLANE)
    far_w = other(own_w, "zl")

    factors, _, far_t = lax.optimization_barrier((factors, own_w, far_t))
    own_f = exchange(factors.reshape(16, 4, 16, 1536), PLANE)
    part = ladder_part(own_f, own_t, far_t, own_w, far_w)
    part = ladder_part(other(own_f, "core"), other(own_t, "core"), other(far_t, "core"), own_w, far_w, part)

    part = sum_parts(exchange(part, PLANE))
    part = jnp.transpose(part.reshape(2, 16, 8, 64), (2, 0, 1, 3))
    part = exchange(part, ("zh", "core"))
    out = jnp.sum(part.reshape(4, 4, 16, 64), axis=0)
    return jnp.transpose(out, (2, 0, 1))


def solution(mesh):
    fine = Mesh(mesh.devices.reshape(4, 2, 4, 4, 2), ("y", "zl", "x", "zh", "core"))
    row, col = ("y", "zl", "x"), ("zh", "core")
    return jax.shard_map(
        per_device,
        mesh=fine,
        in_specs=(P(None, col, row), P(col, row, None), P(None, row, col)),
        out_specs=P(col, None, row),
        check_vma=False,
    )
```

```python
import jax
import jax.numpy as jnp
from jax import lax
from jax.experimental import pallas as pl
from jax.experimental.pallas import tpu as pltpu
from jax.sharding import Mesh
from jax.sharding import PartitionSpec as P

BF16 = jnp.bfloat16
F32 = jnp.float32
PLANE = ("y", "x")
ROW = ("y", "zl", "x")
RING = ("zl", "zh")
MIB = 1024 * 1024


def in_hbm(*arrays):
    return [pltpu.with_memory_space_constraint(a, pltpu.HBM) for a in arrays]


def dot(left, right):
    return lax.dot_general(left, right, (((1,), (0,)), ((), ())), preferred_element_type=F32)


def spread_kernel(own_ref, far_ref, out_ref):
    core = lax.axis_index("core")
    for a in range(2):
        mine, theirs = own_ref[2 * core + a], far_ref[2 * core + a]
        first = jnp.where(core == 0, mine, theirs)
        second = jnp.where(core == 0, theirs, mine)
        block = jnp.concatenate([first, second], axis=-1)
        for s in range(16):
            out_ref[s, a] = block


def spread(own, far):
    return pl.pallas_call(
        spread_kernel,
        out_shape=jax.ShapeDtypeStruct((16, 2, 48, 128), BF16),
        name="spread_window",
    )(own, far)


def regroup_kernel(t_ref, out_ref):
    dest = lax.broadcasted_iota(jnp.int32, (256, 256), 0)
    src = lax.broadcasted_iota(jnp.int32, (256, 256), 1)
    select = jnp.where(src == (dest % 16) * 16 + dest // 16, 1.0, 0.0).astype(BF16)
    rows = dot(select, t_ref[...].reshape(256, 512)).astype(BF16).reshape(4, 4, 16, 512)
    out_ref[0:4] = rows
    out_ref[4:8] = rows


def regroup(amps):
    return pl.pallas_call(
        regroup_kernel,
        out_shape=jax.ShapeDtypeStruct((32, 4, 16, 512), BF16),
        grid=(4,),
        in_specs=[pl.BlockSpec((16, 16, 512), lambda g: (0, g, 0))],
        out_specs=pl.BlockSpec((8, 4, 16, 512), lambda g: (g, 0, 0, 0)),
        name="regroup_amplitudes",
    )(amps)


def integrals_kernel(own_f, far_f, *rest):
    blocks, (own_v, far_v, window) = rest[:-3], rest[-3:]
    g = pl.program_id(0)

    @pl.when(g == 0)
    def _():
        z = 2 * lax.axis_index("zh") + lax.axis_index("zl")
        for step, ref in zip((0, -1, 1, -2, 2, -3, 3, 4, 4), blocks):
            at = (z + step + 8) % 8
            row, lane = (at % 2) * 192, pl.multiple_of((at // 2) * 128, 128)
            count = ref.shape[0] // 4
            first = 2 if ref is blocks[8] else 0
            for y in range(count):
                rows = pl.ds(pl.multiple_of((y + first) * 384 + row, 192), 192)
                for a in range(2):
                    window[a, rows, pl.ds(lane, 128)] = ref[4 * y : 4 * y + 4, a].reshape(192, 128)

    def step(f_ref, out_ref):
        factors = f_ref[...].reshape(512, 1536)
        for a in range(2):
            integrals = dot(factors, window[a]).astype(BF16).reshape(16, 2, 16, 512)
            for d in range(2):
                out_ref[d, a] = integrals[:, d].reshape(256, 512)

    @pl.when(g < 2)
    def _():
        step(own_f, own_v)

    @pl.when(g >= 2)
    def _():
        step(far_f, far_v)


def build_integrals(own_f, far_f, blocks):
    return pl.pallas_call(
        integrals_kernel,
        out_shape=[pltpu.VMEM((4, 2, 256, 512), BF16)] * 2,
        grid=(4,),
        in_specs=[
            pl.BlockSpec((16, 2, 16, 1536), lambda g: (0, jnp.minimum(g, 1), 0, 0)),
            pl.BlockSpec((16, 2, 16, 1536), lambda g: (0, jnp.maximum(g - 2, 0), 0, 0)),
        ]
        + [pl.BlockSpec(b.shape, lambda g: (0, 0, 0, 0)) for b in blocks],
        out_specs=[
            pl.BlockSpec((2, 2, 256, 512), lambda g: (jnp.minimum(g, 1), 0, 0, 0)),
            pl.BlockSpec((2, 2, 256, 512), lambda g: (jnp.maximum(g - 2, 0), 0, 0, 0)),
        ],
        scratch_shapes=[pltpu.VMEM((2, 1536, 512), BF16)],
        compiler_params=pltpu.CompilerParams(vmem_limit_bytes=28 * MIB),
        cost_estimate=pl.CostEstimate(flops=6_500_000_000, bytes_accessed=14_000_000, transcendentals=0),
        name="build_integrals",
    )(own_f, far_f, *in_hbm(*blocks))


def ladder_kernel(t_ref, v_ref, *rest):
    start, out_ref = rest[:-1], rest[-1]
    for a in range(2):
        rows = slice(256 * a, 256 * a + 256)
        total = start[0][rows] if start else 0.0
        for d in range(4):
            total = total + dot(v_ref[d, a], t_ref[:, d].reshape(512, 512))
        if start:
            out_ref[:, a] = total.reshape(16, 16, 512).astype(BF16)
        else:
            out_ref[rows] = total


def ladder_part(*operands):
    out_shape = (16, 2, 16, 512) if len(operands) == 3 else (512, 512)
    return pl.pallas_call(
        ladder_kernel,
        out_shape=jax.ShapeDtypeStruct(out_shape, BF16 if len(operands) == 3 else F32),
        in_specs=[pl.BlockSpec(memory_space=pltpu.VMEM)] * len(operands),
        out_specs=pl.BlockSpec(memory_space=pltpu.VMEM),
        compiler_params=pltpu.CompilerParams(vmem_limit_bytes=16 * MIB),
        cost_estimate=pl.CostEstimate(flops=100_000_000_000, bytes_accessed=5_000_000, transcendentals=0),
        name="ladder_part",
    )(*operands)


def sum_kernel(parts_ref, out_ref):
    total = jnp.sum(parts_ref[...].astype(F32), axis=0)
    for q in range(8):
        lanes = slice(64 * q, 64 * q + 64)
        out_ref[q] = jnp.concatenate([total[0, :, lanes], total[1, :, lanes]], axis=-1)


def sum_parts(parts):
    return pl.pallas_call(
        sum_kernel,
        out_shape=jax.ShapeDtypeStruct((8, 16, 128), F32),
        name="sum_parts",
    )(parts)


def finish_kernel(parts_ref, out_ref):
    for core in range(2):
        both = parts_ref[core] + parts_ref[2 + core] + parts_ref[4 + core] + parts_ref[6 + core]
        out_ref[2 * core] = both[:, :64]
        out_ref[2 * core + 1] = both[:, 64:]


def finish(parts):
    return pl.pallas_call(
        finish_kernel,
        out_shape=jax.ShapeDtypeStruct((4, 16, 64), F32),
        name="finish",
    )(parts)


def exchange(x, axis):
    return lax.all_to_all(x, axis, split_axis=0, concat_axis=0, tiled=True)


def other(x, axis):
    return lax.ppermute(x, axis, [(0, 1), (1, 0)])


def shift(x, step):
    def flat(z):
        return (z % 2) * 4 + (z // 2) % 4

    return lax.ppermute(x, RING, [(flat(z), flat((z + step) % 8)) for z in range(8)])


def per_device(window_factors, factors, amplitudes):
    window = jnp.transpose(window_factors, (0, 2, 1))
    own_w = exchange(spread(window, other(window, "core")), PLANE)
    own_t = regroup(jnp.transpose(amplitudes, (1, 2, 0)))
    factors, own_w, own_t = lax.optimization_barrier((factors, own_w, own_t))
    own_f = exchange(factors.reshape(16, 4, 16, 1536), PLANE)

    blocks, up, down = [own_w], own_w, own_w
    for _ in range(3):
        up, down = shift(up, 1), shift(down, -1)
        blocks += [up, down]
    blocks += [shift(up[:8], 1), shift(down[8:], -1)]
    own_t, own_f, *blocks = lax.optimization_barrier((own_t, own_f, *blocks))
    amps = exchange(own_t, ROW)
    own_v, far_v = build_integrals(own_f, other(own_f, "core"), blocks)
    part = ladder_part(amps, own_v)
    part = ladder_part(other(amps, "core"), far_v, part)

    part = sum_parts(exchange(part, PLANE))
    return jnp.transpose(finish(exchange(part, ("zh", "core"))), (2, 0, 1))


def solution(mesh):
    fine = Mesh(mesh.devices.reshape(4, 2, 4, 4, 2), ("y", "zl", "x", "zh", "core"))
    row, col = ROW, ("zh", "core")
    return jax.shard_map(
        per_device,
        mesh=fine,
        in_specs=(P(None, col, row), P(col, row, None), P(None, row, col)),
        out_specs=P(col, None, row),
        check_vma=False,
    )
```

```python
import jax
import jax.numpy as jnp
from jax import lax
from jax.experimental import pallas as pl
from jax.experimental.pallas import tpu as pltpu
from jax.sharding import Mesh
from jax.sharding import PartitionSpec as P

BF16 = jnp.bfloat16
F32 = jnp.float32
PLANE = ("x", "y")
ROW = ("y", "zl", "x")
RING = ("zl", "zh")
MIB = 1024 * 1024


def in_hbm(*arrays):
    return [pltpu.with_memory_space_constraint(a, pltpu.HBM) for a in arrays]


def dot(left, right):
    return lax.dot_general(left, right, (((1,), (0,)), ((), ())), preferred_element_type=F32)


def spread_kernel(own_ref, far_ref, out_ref):
    core = lax.axis_index("core")
    for a in range(2):
        mine, theirs = own_ref[2 * core + a], far_ref[2 * core + a]
        first = jnp.where(core == 0, mine, theirs)
        second = jnp.where(core == 0, theirs, mine)
        block = jnp.concatenate([first, second], axis=-1)
        for s in range(16):
            out_ref[s, a] = block


def spread(own, far):
    return pl.pallas_call(
        spread_kernel,
        out_shape=jax.ShapeDtypeStruct((16, 2, 48, 128), BF16),
        name="spread_window",
    )(own, far)


def regroup_kernel(t_ref, out_ref):
    dest = lax.broadcasted_iota(jnp.int32, (256, 256), 0)
    src = lax.broadcasted_iota(jnp.int32, (256, 256), 1)
    select = jnp.where(src == (dest % 16) * 16 + dest // 16, 1.0, 0.0).astype(BF16)
    rows = dot(select, t_ref[...].reshape(256, 512)).astype(BF16).reshape(4, 4, 16, 512)
    out_ref[:, 0, 0] = rows
    out_ref[:, 1, 0] = rows


def regroup(amps):
    return pl.pallas_call(
        regroup_kernel,
        out_shape=jax.ShapeDtypeStruct((4, 2, 4, 4, 16, 512), BF16),
        grid=(4,),
        in_specs=[pl.BlockSpec((16, 16, 512), lambda g: (0, g, 0))],
        out_specs=pl.BlockSpec((4, 2, 1, 4, 16, 512), lambda g: (0, 0, g, 0, 0, 0)),
        name="regroup_amplitudes",
    )(amps).reshape(32, 4, 16, 512)


def integrals_kernel(own_f, far_f, *rest):
    blocks, (own_v, far_v, window) = rest[:-3], rest[-3:]
    g = pl.program_id(0)

    @pl.when(g == 0)
    def _():
        z = 2 * lax.axis_index("zh") + lax.axis_index("zl")
        for step, ref in zip((0, -1, 1, -2, 2, -3, 3, 4, 4), blocks):
            at = (z + step + 8) % 8
            row, lane = (at % 2) * 192, pl.multiple_of((at // 2) * 128, 128)
            count = ref.shape[0] // 4
            first = 2 if ref is blocks[8] else 0
            for y in range(count):
                rows = pl.ds(pl.multiple_of((y + first) * 384 + row, 192), 192)
                for a in range(2):
                    window[a, rows, pl.ds(lane, 128)] = ref[4 * y : 4 * y + 4, a].reshape(192, 128)

    def step(f_ref, out_ref):
        factors = f_ref[...].reshape(512, 1536)
        for a in range(2):
            integrals = dot(factors, window[a]).astype(BF16).reshape(16, 2, 16, 512)
            for d in range(2):
                out_ref[d, a] = integrals[:, d].reshape(256, 512)

    @pl.when(g < 2)
    def _():
        step(own_f, own_v)

    @pl.when(g >= 2)
    def _():
        step(far_f, far_v)


def build_integrals(own_f, far_f, blocks):
    return pl.pallas_call(
        integrals_kernel,
        out_shape=[pltpu.VMEM((4, 2, 256, 512), BF16)] * 2,
        grid=(4,),
        in_specs=[
            pl.BlockSpec((16, 2, 16, 1536), lambda g: (0, jnp.minimum(g, 1), 0, 0)),
            pl.BlockSpec((16, 2, 16, 1536), lambda g: (0, jnp.maximum(g - 2, 0), 0, 0)),
        ]
        + [pl.BlockSpec(b.shape, lambda g: (0, 0, 0, 0)) for b in blocks],
        out_specs=[
            pl.BlockSpec((2, 2, 256, 512), lambda g: (jnp.minimum(g, 1), 0, 0, 0)),
            pl.BlockSpec((2, 2, 256, 512), lambda g: (jnp.maximum(g - 2, 0), 0, 0, 0)),
        ],
        scratch_shapes=[pltpu.VMEM((2, 1536, 512), BF16)],
        compiler_params=pltpu.CompilerParams(vmem_limit_bytes=28 * MIB),
        cost_estimate=pl.CostEstimate(flops=6_500_000_000, bytes_accessed=14_000_000, transcendentals=0),
        name="build_integrals",
    )(own_f, far_f, *in_hbm(*blocks))


def ladder_kernel(t_ref, v_ref, *rest):
    start, out_ref = rest[:-1], rest[-1]
    for a in range(2):
        rows = slice(256 * a, 256 * a + 256)
        total = start[0][rows] if start else 0.0
        for d in range(4):
            total = total + dot(v_ref[d, a], t_ref[:, d].reshape(512, 512))
        if start:
            out_ref[:, a] = total.reshape(16, 16, 512).astype(BF16)
        else:
            out_ref[rows] = total


def ladder_part(*operands):
    out_shape = (16, 2, 16, 512) if len(operands) == 3 else (512, 512)
    return pl.pallas_call(
        ladder_kernel,
        out_shape=jax.ShapeDtypeStruct(out_shape, BF16 if len(operands) == 3 else F32),
        in_specs=[pl.BlockSpec(memory_space=pltpu.VMEM)] * len(operands),
        out_specs=pl.BlockSpec(memory_space=pltpu.VMEM),
        compiler_params=pltpu.CompilerParams(vmem_limit_bytes=16 * MIB),
        cost_estimate=pl.CostEstimate(flops=100_000_000_000, bytes_accessed=5_000_000, transcendentals=0),
        name="ladder_part",
    )(*operands)


def sum_kernel(parts_ref, out_ref):
    total = jnp.sum(parts_ref[...].astype(F32), axis=0)
    for q in range(8):
        lanes = slice(64 * q, 64 * q + 64)
        out_ref[q % 2 * 4 + q // 2] = jnp.concatenate([total[0, :, lanes], total[1, :, lanes]], axis=-1)


def sum_parts(parts):
    return pl.pallas_call(
        sum_kernel,
        out_shape=jax.ShapeDtypeStruct((8, 16, 128), F32),
        name="sum_parts",
    )(parts)


def finish_kernel(parts_ref, out_ref):
    for core in range(2):
        both = jnp.sum(parts_ref[4 * core : 4 * core + 4], axis=0)
        out_ref[2 * core] = both[:, :64]
        out_ref[2 * core + 1] = both[:, 64:]


def finish(parts):
    return pl.pallas_call(
        finish_kernel,
        out_shape=jax.ShapeDtypeStruct((4, 16, 64), F32),
        name="finish",
    )(parts)


def exchange(x, axis):
    return lax.all_to_all(x, axis, split_axis=0, concat_axis=0, tiled=True)


def other(x, axis):
    return lax.ppermute(x, axis, [(0, 1), (1, 0)])


def shift(x, step):
    def flat(z):
        return (z % 2) * 4 + (z // 2) % 4

    return lax.ppermute(x, RING, [(flat(z), flat((z + step) % 8)) for z in range(8)])


def per_device(window_factors, factors, amplitudes):
    window = jnp.transpose(window_factors, (0, 2, 1))
    own_w = exchange(spread(window, other(window, "core")), ("y", "x"))
    own_t = regroup(jnp.transpose(amplitudes, (1, 2, 0)))
    factors, own_w, own_t = lax.optimization_barrier((factors, own_w, own_t))
    own_f = exchange(factors.reshape(16, 4, 16, 1536), PLANE)

    blocks, up, down = [own_w], own_w, own_w
    for _ in range(3):
        up, down = shift(up, 1), shift(down, -1)
        blocks += [up, down]
    blocks += [shift(up[:8], 1), shift(down[8:], -1)]
    own_t, own_f, *blocks = lax.optimization_barrier((own_t, own_f, *blocks))
    amps = exchange(own_t, ROW)
    own_v, far_v = build_integrals(own_f, other(own_f, "core"), blocks)
    part = ladder_part(amps, own_v)
    part = ladder_part(other(amps, "core"), far_v, part)

    part = sum_parts(exchange(part, PLANE))
    return jnp.transpose(finish(exchange(part, ("core", "zh"))), (2, 0, 1))


def solution(mesh):
    fine = Mesh(mesh.devices.reshape(4, 2, 4, 4, 2), ("y", "zl", "x", "zh", "core"))
    row, col = ROW, ("zh", "core")
    return jax.shard_map(
        per_device,
        mesh=fine,
        in_specs=(P(None, col, row), P(col, row, None), P(None, row, col)),
        out_specs=P(col, None, row),
        check_vma=False,
    )
```

```python
import jax
import jax.numpy as jnp
from jax import lax
from jax.experimental import pallas as pl
from jax.experimental.pallas import tpu as pltpu
from jax.sharding import Mesh
from jax.sharding import PartitionSpec as P

BF16 = jnp.bfloat16
F32 = jnp.float32
PLANE = ("x", "y")
ROW = ("y", "zl", "x")
RING = ("zl", "zh")
MIB = 1024 * 1024


def in_hbm(*arrays):
    return [pltpu.with_memory_space_constraint(a, pltpu.HBM) for a in arrays]


def dot(left, right):
    return lax.dot_general(left, right, (((1,), (0,)), ((), ())), preferred_element_type=F32)


def spread_kernel(own_ref, far_ref, out_ref):
    core = lax.axis_index("core")
    for a in range(2):
        mine, theirs = own_ref[2 * core + a], far_ref[2 * core + a]
        first = jnp.where(core == 0, mine, theirs)
        second = jnp.where(core == 0, theirs, mine)
        block = jnp.concatenate([first, second], axis=-1)
        for s in range(16):
            out_ref[s, a] = block


def spread(own, far):
    return pl.pallas_call(
        spread_kernel,
        out_shape=jax.ShapeDtypeStruct((16, 2, 48, 128), BF16),
        in_specs=[pl.BlockSpec((4, 48, 64)), pl.BlockSpec(memory_space=pltpu.VMEM)],
        name="spread_window",
    )(*in_hbm(own), far)


def regroup_kernel(t_ref, out_ref):
    dest = lax.broadcasted_iota(jnp.int32, (256, 256), 0)
    src = lax.broadcasted_iota(jnp.int32, (256, 256), 1)
    select = jnp.where(src == (dest % 16) * 16 + dest // 16, 1.0, 0.0).astype(BF16)
    rows = dot(select, t_ref[...].reshape(256, 512)).astype(BF16).reshape(4, 4, 16, 512)
    out_ref[:, 0, 0] = rows
    out_ref[:, 1, 0] = rows


def regroup(amps):
    return pl.pallas_call(
        regroup_kernel,
        out_shape=jax.ShapeDtypeStruct((4, 2, 4, 4, 16, 512), BF16),
        grid=(4,),
        in_specs=[pl.BlockSpec((16, 16, 512), lambda g: (0, g, 0))],
        out_specs=pl.BlockSpec((4, 2, 1, 4, 16, 512), lambda g: (0, 0, g, 0, 0, 0)),
        name="regroup_amplitudes",
    )(amps).reshape(32, 4, 16, 512)


def integrals_kernel(own_f, far_f, *rest):
    blocks, (own_v, far_v, window) = rest[:-3], rest[-3:]
    g = pl.program_id(0)

    @pl.when(g == 0)
    def _():
        z = 2 * lax.axis_index("zh") + lax.axis_index("zl")
        for step, ref in zip((0, -1, 1, -2, 2, -3, 3, 4, 4), blocks):
            at = (z + step + 8) % 8
            row, lane = (at % 2) * 192, pl.multiple_of((at // 2) * 128, 128)
            count = ref.shape[0] // 4
            first = 2 if ref is blocks[8] else 0
            for y in range(count):
                rows = pl.ds(pl.multiple_of((y + first) * 384 + row, 192), 192)
                for a in range(2):
                    window[a, rows, pl.ds(lane, 128)] = ref[4 * y : 4 * y + 4, a].reshape(192, 128)

    def step(f_ref, out_ref):
        factors = f_ref[...].reshape(512, 1536)
        for a in range(2):
            integrals = dot(factors, window[a]).astype(BF16).reshape(16, 2, 16, 512)
            for d in range(2):
                out_ref[d, a] = integrals[:, d].reshape(256, 512)

    @pl.when(g < 2)
    def _():
        step(own_f, own_v)

    @pl.when(g >= 2)
    def _():
        step(far_f, far_v)


def build_integrals(own_f, far_f, blocks):
    return pl.pallas_call(
        integrals_kernel,
        out_shape=[pltpu.HBM((4, 2, 256, 512), BF16)] * 2,
        grid=(4,),
        in_specs=[
            pl.BlockSpec((16, 2, 16, 1536), lambda g: (0, jnp.minimum(g, 1), 0, 0)),
            pl.BlockSpec((16, 2, 16, 1536), lambda g: (0, jnp.maximum(g - 2, 0), 0, 0)),
        ]
        + [pl.BlockSpec(b.shape, lambda g: (0, 0, 0, 0)) for b in blocks],
        out_specs=[
            pl.BlockSpec((2, 2, 256, 512), lambda g: (jnp.minimum(g, 1), 0, 0, 0)),
            pl.BlockSpec((2, 2, 256, 512), lambda g: (jnp.maximum(g - 2, 0), 0, 0, 0)),
        ],
        scratch_shapes=[pltpu.VMEM((2, 1536, 512), BF16)],
        compiler_params=pltpu.CompilerParams(vmem_limit_bytes=28 * MIB),
        cost_estimate=pl.CostEstimate(flops=6_500_000_000, bytes_accessed=14_000_000, transcendentals=0),
        name="build_integrals",
    )(own_f, far_f, *in_hbm(*blocks))


def ladder_kernel(t_ref, v_ref, *rest):
    start, out_ref = rest[:-1], rest[-1]
    for a in range(2):
        rows = slice(256 * a, 256 * a + 256)
        total = start[0][rows] if start else 0.0
        for d in range(4):
            total = total + dot(v_ref[d, a], t_ref[:, d].reshape(512, 512))
        if start:
            out_ref[:, a] = total.reshape(16, 16, 512).astype(BF16)
        else:
            out_ref[rows] = total


def first_kernel(t_ref, v_ref, out_ref, amps, integrals, sems):
    copies = []
    for d in range(4):
        pair = (
            pltpu.make_async_copy(t_ref.at[:, d], amps.at[d], sems.at[0, d]),
            pltpu.make_async_copy(v_ref.at[d], integrals.at[d], sems.at[1, d]),
        )
        for copy in pair:
            copy.start()
        copies.append(pair)
    for d, pair in enumerate(copies):
        for copy in pair:
            copy.wait()
        product = dot(integrals[d].reshape(512, 512), amps[d].reshape(512, 512))
        out_ref[...] = product + out_ref[...] if d else product


def first_part(amps, integrals):
    return pl.pallas_call(
        first_kernel,
        out_shape=jax.ShapeDtypeStruct((512, 512), F32),
        in_specs=[pl.BlockSpec(memory_space=pl.ANY)] * 2,
        out_specs=pl.BlockSpec(memory_space=pltpu.VMEM),
        scratch_shapes=[
            pltpu.VMEM((4, 32, 16, 512), BF16),
            pltpu.VMEM((4, 2, 256, 512), BF16),
            pltpu.SemaphoreType.DMA((2, 4)),
        ],
        compiler_params=pltpu.CompilerParams(vmem_limit_bytes=16 * MIB),
        cost_estimate=pl.CostEstimate(flops=100_000_000_000, bytes_accessed=5_000_000, transcendentals=0),
        name="first_part",
    )(amps, *in_hbm(integrals))


def ladder_part(*operands):
    out_shape = (16, 2, 16, 512) if len(operands) == 3 else (512, 512)
    return pl.pallas_call(
        ladder_kernel,
        out_shape=jax.ShapeDtypeStruct(out_shape, BF16 if len(operands) == 3 else F32),
        in_specs=[pl.BlockSpec(memory_space=pltpu.VMEM)] * len(operands),
        out_specs=pl.BlockSpec(memory_space=pltpu.VMEM),
        compiler_params=pltpu.CompilerParams(vmem_limit_bytes=16 * MIB),
        cost_estimate=pl.CostEstimate(flops=100_000_000_000, bytes_accessed=5_000_000, transcendentals=0),
        name="ladder_part",
    )(*operands)


def sum_kernel(parts_ref, out_ref):
    total = jnp.sum(parts_ref[...].astype(F32), axis=0)
    for q in range(8):
        lanes = slice(64 * q, 64 * q + 64)
        out_ref[q % 2 * 4 + q // 2] = jnp.concatenate([total[0, :, lanes], total[1, :, lanes]], axis=-1)


def sum_parts(parts):
    return pl.pallas_call(
        sum_kernel,
        out_shape=jax.ShapeDtypeStruct((8, 16, 128), F32),
        name="sum_parts",
    )(parts)


def exchange(x, axis):
    return lax.all_to_all(x, axis, split_axis=0, concat_axis=0, tiled=True)


def other(x, axis):
    return lax.ppermute(x, axis, [(0, 1), (1, 0)])


def shift(x, step):
    def flat(z):
        return (z % 2) * 4 + (z // 2) % 4

    return lax.ppermute(x, RING, [(flat(z), flat((z + step) % 8)) for z in range(8)])


def per_device(window_factors, factors, amplitudes):
    window = jnp.transpose(window_factors, (0, 2, 1))
    own_w = exchange(spread(window, other(window, "core")), ("y", "x"))
    own_t = regroup(jnp.transpose(amplitudes, (1, 2, 0)))
    factors, own_w, own_t = lax.optimization_barrier((factors, own_w, own_t))
    own_f = exchange(factors.reshape(16, 64, 1536), PLANE).reshape(16, 4, 16, 1536)

    blocks, up, down = [own_w], own_w, own_w
    for _ in range(3):
        up, down = shift(up, 1), shift(down, -1)
        blocks += [up, down]
    blocks += [shift(up[:8], 1), shift(down[8:], -1)]
    own_t, own_f, *blocks = lax.optimization_barrier((own_t, own_f, *blocks))
    amps = exchange(own_t.reshape(32, 64, 512), ROW).reshape(32, 4, 16, 512)
    own_v, far_v = build_integrals(own_f, other(own_f, "core"), blocks)
    part = first_part(amps, own_v)
    part = ladder_part(other(amps, "core"), far_v, part)

    part = sum_parts(exchange(part, PLANE))
    part = exchange(part, ("core", "zh")).reshape(2, 4, 16, 2, 64)
    return jnp.transpose(jnp.sum(part, axis=1), (3, 0, 2, 1)).reshape(64, 4, 16)


def solution(mesh):
    fine = Mesh(mesh.devices.reshape(4, 2, 4, 4, 2), ("y", "zl", "x", "zh", "core"))
    row, col = ROW, ("zh", "core")
    return jax.shard_map(
        per_device,
        mesh=fine,
        in_specs=(P(None, col, row), P(col, row, None), P(None, row, col)),
        out_specs=P(col, None, row),
        check_vma=False,
    )
```

```python
import jax
import jax.numpy as jnp
from jax import lax
from jax.experimental import pallas as pl
from jax.experimental.pallas import tpu as pltpu
from jax.sharding import Mesh
from jax.sharding import PartitionSpec as P

BF16 = jnp.bfloat16
F32 = jnp.float32
PLANE = ("x", "y")
ROW = ("y", "zl", "x")
RING = ("zl", "zh")
MIB = 1024 * 1024


def in_hbm(*arrays):
    return [pltpu.with_memory_space_constraint(a, pltpu.HBM) for a in arrays]


def dot(left, right):
    return lax.dot_general(left, right, (((1,), (0,)), ((), ())), preferred_element_type=F32)


def spread_kernel(w_ref, out_ref):
    for half in range(2):
        block = jnp.concatenate([w_ref[2 * half], w_ref[2 * half + 1]], axis=-1)
        for s in range(16):
            out_ref[s, half] = block


def spread(window):
    return pl.pallas_call(
        spread_kernel,
        out_shape=jax.ShapeDtypeStruct((16, 2, 48, 128), BF16),
        name="spread_window",
    )(*in_hbm(window))


def join_kernel(own_ref, far_ref, *out_refs):
    core = lax.axis_index("core")
    mine, theirs = own_ref[:, core], far_ref[:, core]
    first = jnp.where(core == 0, mine, theirs)
    second = jnp.where(core == 0, theirs, mine)
    for a in range(2):
        lanes = slice(64 * a, 64 * a + 64)
        block = jnp.concatenate([first[..., lanes], second[..., lanes]], axis=-1)
        out_refs[0][:, a] = block[:8]
        out_refs[1][:, a] = block[8:]


def join_cores(own, far):
    return pl.pallas_call(
        join_kernel,
        out_shape=[jax.ShapeDtypeStruct((8, 2, 48, 128), BF16)] * 2,
        name="join_window",
    )(own, far)


def regroup_kernel(t_ref, out_ref):
    dest = lax.broadcasted_iota(jnp.int32, (256, 256), 0)
    src = lax.broadcasted_iota(jnp.int32, (256, 256), 1)
    select = jnp.where(src == (dest % 16) * 16 + dest // 16, 1.0, 0.0).astype(BF16)
    rows = dot(select, t_ref[...].reshape(256, 512)).astype(BF16).reshape(4, 4, 16, 512)
    out_ref[:, 0, 0] = rows
    out_ref[:, 1, 0] = rows


def regroup(amps):
    return pl.pallas_call(
        regroup_kernel,
        out_shape=jax.ShapeDtypeStruct((4, 2, 4, 4, 16, 512), BF16),
        grid=(4,),
        in_specs=[pl.BlockSpec((16, 16, 512), lambda g: (0, g, 0))],
        out_specs=pl.BlockSpec((4, 2, 1, 4, 16, 512), lambda g: (0, 0, g, 0, 0, 0)),
        name="regroup_amplitudes",
    )(amps).reshape(32, 4, 16, 512)


def integrals_kernel(own_f, far_f, *rest):
    blocks, (own_v, far_v, window) = rest[:-3], rest[-3:]
    g = pl.program_id(0)

    @pl.when(g == 0)
    def _():
        z = 2 * lax.axis_index("zh") + lax.axis_index("zl")
        for n, ref in enumerate(blocks):
            at = (z + (0, -1, 1, -2, 2, -3, 3, 4)[n // 2] + 8) % 8
            row, lane = (at % 2) * 192, pl.multiple_of((at // 2) * 128, 128)
            for y in range(2):
                rows = pl.ds(pl.multiple_of((y + n % 2 * 2) * 384 + row, 192), 192)
                for a in range(2):
                    window[a, rows, pl.ds(lane, 128)] = ref[4 * y : 4 * y + 4, a].reshape(192, 128)

    def step(f_ref, out_ref):
        factors = f_ref[...].reshape(512, 1536)
        for a in range(2):
            integrals = dot(factors, window[a]).astype(BF16).reshape(16, 2, 16, 512)
            for d in range(2):
                out_ref[d, a] = integrals[:, d].reshape(256, 512)

    @pl.when(g < 2)
    def _():
        step(own_f, own_v)

    @pl.when(g >= 2)
    def _():
        step(far_f, far_v)


def build_integrals(own_f, far_f, blocks):
    return pl.pallas_call(
        integrals_kernel,
        out_shape=[pltpu.HBM((4, 2, 256, 512), BF16)] * 2,
        grid=(4,),
        in_specs=[
            pl.BlockSpec((16, 2, 16, 1536), lambda g: (0, jnp.minimum(g, 1), 0, 0)),
            pl.BlockSpec((16, 2, 16, 1536), lambda g: (0, jnp.maximum(g - 2, 0), 0, 0)),
        ]
        + [pl.BlockSpec(b.shape, lambda g: (0, 0, 0, 0)) for b in blocks],
        out_specs=[
            pl.BlockSpec((2, 2, 256, 512), lambda g: (jnp.minimum(g, 1), 0, 0, 0)),
            pl.BlockSpec((2, 2, 256, 512), lambda g: (jnp.maximum(g - 2, 0), 0, 0, 0)),
        ],
        scratch_shapes=[pltpu.VMEM((2, 1536, 512), BF16)],
        compiler_params=pltpu.CompilerParams(vmem_limit_bytes=28 * MIB),
        cost_estimate=pl.CostEstimate(flops=6_500_000_000, bytes_accessed=14_000_000, transcendentals=0),
        name="build_integrals",
    )(own_f, far_f, *in_hbm(*blocks))


def ladder_kernel(t_ref, v_ref, *rest):
    start, out_ref = rest[:-1], rest[-1]
    for a in range(2):
        rows = slice(256 * a, 256 * a + 256)
        total = start[0][rows] if start else 0.0
        for d in range(4):
            total = total + dot(v_ref[d, a], t_ref[:, d].reshape(512, 512))
        if start:
            out_ref[:, a] = total.reshape(16, 16, 512).astype(BF16)
        else:
            out_ref[rows] = total


def first_kernel(t_ref, v_ref, out_ref, amps, integrals, sems):
    copies = []
    for d in range(4):
        pair = (
            pltpu.make_async_copy(t_ref.at[:, d], amps.at[d], sems.at[0, d]),
            pltpu.make_async_copy(v_ref.at[d], integrals.at[d], sems.at[1, d]),
        )
        for copy in pair:
            copy.start()
        copies.append(pair)
    for d, pair in enumerate(copies):
        for copy in pair:
            copy.wait()
        product = dot(integrals[d].reshape(512, 512), amps[d].reshape(512, 512))
        out_ref[...] = product + out_ref[...] if d else product


def first_part(amps, integrals):
    return pl.pallas_call(
        first_kernel,
        out_shape=jax.ShapeDtypeStruct((512, 512), F32),
        in_specs=[pl.BlockSpec(memory_space=pl.ANY)] * 2,
        out_specs=pl.BlockSpec(memory_space=pltpu.VMEM),
        scratch_shapes=[
            pltpu.VMEM((4, 32, 16, 512), BF16),
            pltpu.VMEM((4, 2, 256, 512), BF16),
            pltpu.SemaphoreType.DMA((2, 4)),
        ],
        compiler_params=pltpu.CompilerParams(vmem_limit_bytes=16 * MIB),
        cost_estimate=pl.CostEstimate(flops=100_000_000_000, bytes_accessed=5_000_000, transcendentals=0),
        name="first_part",
    )(amps, *in_hbm(integrals))


def ladder_part(*operands):
    out_shape = (16, 2, 16, 512) if len(operands) == 3 else (512, 512)
    return pl.pallas_call(
        ladder_kernel,
        out_shape=jax.ShapeDtypeStruct(out_shape, BF16 if len(operands) == 3 else F32),
        in_specs=[pl.BlockSpec(memory_space=pltpu.VMEM)] * len(operands),
        out_specs=pl.BlockSpec(memory_space=pltpu.VMEM),
        compiler_params=pltpu.CompilerParams(vmem_limit_bytes=16 * MIB),
        cost_estimate=pl.CostEstimate(flops=100_000_000_000, bytes_accessed=5_000_000, transcendentals=0),
        name="ladder_part",
    )(*operands)


def sum_kernel(parts_ref, out_ref):
    total = jnp.sum(parts_ref[...].astype(F32), axis=0)
    for q in range(8):
        lanes = slice(64 * q, 64 * q + 64)
        out_ref[q % 2 * 4 + q // 2] = jnp.concatenate([total[0, :, lanes], total[1, :, lanes]], axis=-1)


def sum_parts(parts):
    return pl.pallas_call(
        sum_kernel,
        out_shape=jax.ShapeDtypeStruct((8, 16, 128), F32),
        name="sum_parts",
    )(parts)


def exchange(x, axis):
    return lax.all_to_all(x, axis, split_axis=0, concat_axis=0, tiled=True)


def other(x, axis):
    return lax.ppermute(x, axis, [(0, 1), (1, 0)])


def shift(x, step):
    def flat(z):
        return (z % 2) * 4 + (z // 2) % 4

    return lax.ppermute(x, RING, [(flat(z), flat((z + step) % 8)) for z in range(8)])


def per_device(window_factors, factors, amplitudes):
    window = jnp.transpose(window_factors, (0, 2, 1))
    own_w = exchange(spread(window), ("y", "x"))
    own_t = regroup(jnp.transpose(amplitudes, (1, 2, 0)))
    factors, own_w, own_t = lax.optimization_barrier((factors, own_w, own_t))
    own_f = exchange(factors.reshape(16, 64, 1536), PLANE).reshape(16, 4, 16, 1536)

    up = down = join_cores(own_w, other(own_w, "core"))
    blocks = list(up)
    for _ in range(3):
        up, down = [shift(half, 1) for half in up], [shift(half, -1) for half in down]
        blocks += up + down
    blocks += [shift(up[0], 1), shift(down[1], -1)]
    own_t, own_f, *blocks = lax.optimization_barrier((own_t, own_f, *blocks))
    amps = exchange(own_t.reshape(32, 64, 512), ROW).reshape(32, 4, 16, 512)
    own_v, far_v = build_integrals(own_f, other(own_f, "core"), blocks)
    part = first_part(amps, own_v)
    part = ladder_part(other(amps, "core"), far_v, part)

    part = sum_parts(exchange(part, PLANE))
    part = exchange(part, ("core", "zh")).reshape(2, 4, 16, 2, 64)
    return jnp.transpose(jnp.sum(part, axis=1), (3, 0, 2, 1)).reshape(64, 4, 16)


def solution(mesh):
    fine = Mesh(mesh.devices.reshape(4, 2, 4, 4, 2), ("y", "zl", "x", "zh", "core"))
    row, col = ROW, ("zh", "core")
    return jax.shard_map(
        per_device,
        mesh=fine,
        in_specs=(P(None, col, row), P(col, row, None), P(None, row, col)),
        out_specs=P(col, None, row),
        check_vma=False,
    )
```

```python
import jax
import jax.numpy as jnp
from jax import lax
from jax.experimental import pallas as pl
from jax.experimental.pallas import tpu as pltpu
from jax.sharding import Mesh
from jax.sharding import PartitionSpec as P

BF16 = jnp.bfloat16
F32 = jnp.float32
PLANE = ("x", "y")
ROW = ("y", "zl", "x")
RING = ("zl", "zh")
MIB = 1024 * 1024


def in_vmem(*arrays):
    return [pltpu.with_memory_space_constraint(a, pltpu.VMEM) for a in arrays]


def in_hbm(*arrays):
    return [pltpu.with_memory_space_constraint(a, pltpu.HBM) for a in arrays]


def dot(left, right):
    return lax.dot_general(left, right, (((1,), (0,)), ((), ())), preferred_element_type=F32)


def spread_kernel(w_ref, out_ref):
    for half in range(2):
        block = jnp.concatenate([w_ref[2 * half], w_ref[2 * half + 1]], axis=-1)
        for s in range(16):
            out_ref[s, half] = block


def spread(window):
    return pl.pallas_call(
        spread_kernel,
        out_shape=pltpu.VMEM((16, 2, 48, 128), BF16),
        name="spread_window",
    )(*in_hbm(window))


def join_kernel(own_ref, far_ref, *out_refs):
    core = lax.axis_index("core")
    mine, theirs = own_ref[:, core], far_ref[:, core]
    first = jnp.where(core == 0, mine, theirs)
    second = jnp.where(core == 0, theirs, mine)
    for a in range(2):
        lanes = slice(64 * a, 64 * a + 64)
        block = jnp.concatenate([first[..., lanes], second[..., lanes]], axis=-1)
        out_refs[0][:, a] = block[:8]
        out_refs[1][:, a] = block[8:]


def join_cores(own, far):
    return pl.pallas_call(
        join_kernel,
        out_shape=[pltpu.VMEM((8, 2, 48, 128), BF16)] * 2,
        name="join_window",
    )(*in_vmem(own, far))


def regroup_kernel(t_ref, out_ref):
    dest = lax.broadcasted_iota(jnp.int32, (256, 256), 0)
    src = lax.broadcasted_iota(jnp.int32, (256, 256), 1)
    select = jnp.where(src == (dest % 16) * 16 + dest // 16, 1.0, 0.0).astype(BF16)
    rows = dot(select, t_ref[...].reshape(256, 512)).astype(BF16).reshape(4, 4, 16, 512)
    out_ref[:, 0, 0] = rows
    out_ref[:, 1, 0] = rows


def regroup(amps):
    return pl.pallas_call(
        regroup_kernel,
        out_shape=jax.ShapeDtypeStruct((4, 2, 4, 4, 16, 512), BF16),
        grid=(4,),
        in_specs=[pl.BlockSpec((16, 16, 512), lambda g: (0, g, 0))],
        out_specs=pl.BlockSpec((4, 2, 1, 4, 16, 512), lambda g: (0, 0, g, 0, 0, 0)),
        name="regroup_amplitudes",
    )(amps).reshape(32, 4, 16, 512)


def integrals_kernel(own_f, far_f, *rest):
    blocks, (own_v, far_v, window) = rest[:-3], rest[-3:]
    g = pl.program_id(0)

    @pl.when(g == 0)
    def _():
        z = 2 * lax.axis_index("zh") + lax.axis_index("zl")
        for n, ref in enumerate(blocks):
            at = (z + (0, -1, 1, -2, 2, -3, 3, 4)[n // 2] + 8) % 8
            row, lane = (at % 2) * 192, pl.multiple_of((at // 2) * 128, 128)
            for y in range(2):
                rows = pl.ds(pl.multiple_of((y + n % 2 * 2) * 384 + row, 192), 192)
                for a in range(2):
                    window[a, rows, pl.ds(lane, 128)] = ref[4 * y : 4 * y + 4, a].reshape(192, 128)

    def step(f_ref, out_ref):
        factors = f_ref[...].reshape(512, 1536)
        for a in range(2):
            integrals = dot(factors, window[a]).astype(BF16).reshape(16, 2, 16, 512)
            for d in range(2):
                out_ref[d, a] = integrals[:, d].reshape(256, 512)

    @pl.when(g < 2)
    def _():
        step(own_f, own_v)

    @pl.when(g >= 2)
    def _():
        step(far_f, far_v)


def build_integrals(own_f, far_f, blocks):
    return pl.pallas_call(
        integrals_kernel,
        out_shape=[pltpu.VMEM((4, 2, 256, 512), BF16)] * 2,
        grid=(4,),
        in_specs=[
            pl.BlockSpec((16, 2, 16, 1536), lambda g: (0, jnp.minimum(g, 1), 0, 0)),
            pl.BlockSpec((16, 2, 16, 1536), lambda g: (0, jnp.maximum(g - 2, 0), 0, 0)),
        ]
        + [pl.BlockSpec(b.shape, lambda g: (0, 0, 0, 0)) for b in blocks],
        out_specs=[
            pl.BlockSpec((2, 2, 256, 512), lambda g: (jnp.minimum(g, 1), 0, 0, 0)),
            pl.BlockSpec((2, 2, 256, 512), lambda g: (jnp.maximum(g - 2, 0), 0, 0, 0)),
        ],
        scratch_shapes=[pltpu.VMEM((2, 1536, 512), BF16)],
        compiler_params=pltpu.CompilerParams(vmem_limit_bytes=28 * MIB),
        cost_estimate=pl.CostEstimate(flops=6_500_000_000, bytes_accessed=14_000_000, transcendentals=0),
        name="build_integrals",
    )(own_f, far_f, *in_hbm(*blocks))


def ladder_kernel(t_ref, v_ref, *rest):
    start, out_ref = rest[:-1], rest[-1]
    for a in range(2):
        rows = slice(256 * a, 256 * a + 256)
        total = start[0][rows] if start else 0.0
        for d in range(4):
            total = total + dot(v_ref[d, a], t_ref[:, d].reshape(512, 512))
        if start:
            out_ref[:, a] = total.reshape(16, 16, 512).astype(BF16)
        else:
            out_ref[rows] = total


def ladder_part(*operands):
    out_shape = (16, 2, 16, 512) if len(operands) == 3 else (512, 512)
    return pl.pallas_call(
        ladder_kernel,
        out_shape=jax.ShapeDtypeStruct(out_shape, BF16 if len(operands) == 3 else F32),
        in_specs=[pl.BlockSpec(memory_space=pltpu.VMEM)] * len(operands),
        out_specs=pl.BlockSpec(memory_space=pltpu.VMEM),
        compiler_params=pltpu.CompilerParams(vmem_limit_bytes=16 * MIB),
        cost_estimate=pl.CostEstimate(flops=100_000_000_000, bytes_accessed=5_000_000, transcendentals=0),
        name="ladder_part",
    )(*in_vmem(*operands))


def sum_kernel(parts_ref, out_ref):
    total = jnp.sum(parts_ref[...].astype(F32), axis=0)
    for q in range(8):
        lanes = slice(64 * q, 64 * q + 64)
        out_ref[q % 2 * 4 + q // 2] = jnp.concatenate([total[0, :, lanes], total[1, :, lanes]], axis=-1)


def sum_parts(parts):
    return pl.pallas_call(
        sum_kernel,
        out_shape=pltpu.VMEM((8, 16, 128), F32),
        name="sum_parts",
    )(*in_vmem(parts))


def exchange(x, axis):
    return lax.all_to_all(x, axis, split_axis=0, concat_axis=0, tiled=True)


def other(x, axis):
    return lax.ppermute(x, axis, [(0, 1), (1, 0)])


def shift(x, step):
    def flat(z):
        return (z % 2) * 4 + (z // 2) % 4

    return lax.ppermute(x, RING, [(flat(z), flat((z + step) % 8)) for z in range(8)])


def per_device(window_factors, factors, amplitudes):
    window = jnp.transpose(window_factors, (0, 2, 1))
    own_w = exchange(spread(window), ("y", "x"))
    own_t = regroup(jnp.transpose(amplitudes, (1, 2, 0)))
    factors, own_w, own_t = lax.optimization_barrier((factors, own_w, own_t))
    own_f = exchange(factors.reshape(16, 64, 1536), PLANE).reshape(16, 4, 16, 1536)

    up = down = join_cores(own_w, other(own_w, "core"))
    blocks = list(up)
    for _ in range(3):
        up, down = [shift(half, 1) for half in up], [shift(half, -1) for half in down]
        blocks += up + down
    blocks += [shift(up[0], 1), shift(down[1], -1)]
    own_t, own_f, *blocks = lax.optimization_barrier((own_t, own_f, *blocks))
    amps = exchange(own_t.reshape(32, 64, 512), ROW).reshape(32, 4, 16, 512)
    own_v, far_v = build_integrals(own_f, other(own_f, "core"), blocks)
    part = ladder_part(amps, own_v)
    part = ladder_part(other(amps, "core"), far_v, part)

    part = sum_parts(exchange(part, PLANE))
    part = exchange(part, ("core", "zh")).reshape(2, 4, 16, 2, 64)
    return jnp.transpose(jnp.sum(part, axis=1), (3, 0, 2, 1)).reshape(64, 4, 16)


def solution(mesh):
    fine = Mesh(mesh.devices.reshape(4, 2, 4, 4, 2), ("y", "zl", "x", "zh", "core"))
    row, col = ROW, ("zh", "core")
    return jax.shard_map(
        per_device,
        mesh=fine,
        in_specs=(P(None, col, row), P(col, row, None), P(None, row, col)),
        out_specs=P(col, None, row),
        check_vma=False,
    )
```

```python
import jax
import jax.numpy as jnp
from jax import lax
from jax.experimental import pallas as pl
from jax.experimental.pallas import tpu as pltpu
from jax.sharding import Mesh
from jax.sharding import PartitionSpec as P

BF16 = jnp.bfloat16
F32 = jnp.float32
PLANE = ("x", "y")
ROW = ("y", "zl", "x")
RING = ("zl", "zh")
MIB = 1024 * 1024


def in_vmem(*arrays):
    return [pltpu.with_memory_space_constraint(a, pltpu.VMEM) for a in arrays]


def in_hbm(*arrays):
    return [pltpu.with_memory_space_constraint(a, pltpu.HBM) for a in arrays]


def dot(left, right):
    return lax.dot_general(left, right, (((1,), (0,)), ((), ())), preferred_element_type=F32)


def spread_kernel(w_ref, out_ref):
    for half in range(2):
        block = jnp.concatenate([w_ref[2 * half], w_ref[2 * half + 1]], axis=-1)
        for s in range(16):
            out_ref[s, half] = block


def spread(window):
    return pl.pallas_call(
        spread_kernel,
        out_shape=pltpu.VMEM((16, 2, 48, 128), BF16),
        name="spread_window",
    )(*in_vmem(window))


def join_kernel(own_ref, far_ref, *out_refs):
    core = lax.axis_index("core")
    mine, theirs = own_ref[:, core], far_ref[:, core]
    first = jnp.where(core == 0, mine, theirs)
    second = jnp.where(core == 0, theirs, mine)
    for a in range(2):
        lanes = slice(64 * a, 64 * a + 64)
        block = jnp.concatenate([first[..., lanes], second[..., lanes]], axis=-1)
        out_refs[0][:, a] = block[:8]
        out_refs[1][:, a] = block[8:]


def join_cores(own, far):
    return pl.pallas_call(
        join_kernel,
        out_shape=[pltpu.VMEM((8, 2, 48, 128), BF16)] * 2,
        name="join_window",
    )(*in_vmem(own, far))


def regroup_kernel(t_ref, out_ref):
    dest = lax.broadcasted_iota(jnp.int32, (256, 256), 0)
    src = lax.broadcasted_iota(jnp.int32, (256, 256), 1)
    select = jnp.where(src == (dest % 16) * 16 + dest // 16, 1.0, 0.0).astype(BF16)
    rows = dot(select, t_ref[...].reshape(256, 512)).astype(BF16).reshape(4, 4, 16, 512)
    out_ref[:, 0, 0] = rows
    out_ref[:, 1, 0] = rows


def regroup(amps):
    return pl.pallas_call(
        regroup_kernel,
        out_shape=jax.ShapeDtypeStruct((4, 2, 4, 4, 16, 512), BF16),
        grid=(4,),
        in_specs=[pl.BlockSpec((16, 16, 512), lambda g: (0, g, 0))],
        out_specs=pl.BlockSpec((4, 2, 1, 4, 16, 512), lambda g: (0, 0, g, 0, 0, 0)),
        name="regroup_amplitudes",
    )(amps).reshape(32, 4, 16, 512)


def integrals_kernel(own_f, far_f, *rest):
    blocks, (own_v, far_v, window) = rest[:-3], rest[-3:]
    g = pl.program_id(0)

    @pl.when(g == 0)
    def _():
        z = 2 * lax.axis_index("zh") + lax.axis_index("zl")
        for n, ref in enumerate(blocks):
            at = (z + (0, -1, 1, -2, 2, -3, 3, 4)[n // 2] + 8) % 8
            row, lane = (at % 2) * 192, pl.multiple_of((at // 2) * 128, 128)
            for y in range(2):
                rows = pl.ds(pl.multiple_of((y + n % 2 * 2) * 384 + row, 192), 192)
                for a in range(2):
                    window[a, rows, pl.ds(lane, 128)] = ref[4 * y : 4 * y + 4, a].reshape(192, 128)

    def step(f_ref, out_ref):
        factors = f_ref[...].reshape(512, 1536)
        for a in range(2):
            integrals = dot(factors, window[a]).astype(BF16).reshape(16, 2, 16, 512)
            for d in range(2):
                out_ref[d, a] = integrals[:, d].reshape(256, 512)

    @pl.when(g < 2)
    def _():
        step(own_f, own_v)

    @pl.when(g >= 2)
    def _():
        step(far_f, far_v)


def build_integrals(own_f, far_f, blocks):
    return pl.pallas_call(
        integrals_kernel,
        out_shape=[pltpu.VMEM((4, 2, 256, 512), BF16)] * 2,
        grid=(4,),
        in_specs=[
            pl.BlockSpec((16, 2, 16, 1536), lambda g: (0, jnp.minimum(g, 1), 0, 0)),
            pl.BlockSpec((16, 2, 16, 1536), lambda g: (0, jnp.maximum(g - 2, 0), 0, 0)),
        ]
        + [pl.BlockSpec(b.shape, lambda g: (0, 0, 0, 0)) for b in blocks],
        out_specs=[
            pl.BlockSpec((2, 2, 256, 512), lambda g: (jnp.minimum(g, 1), 0, 0, 0)),
            pl.BlockSpec((2, 2, 256, 512), lambda g: (jnp.maximum(g - 2, 0), 0, 0, 0)),
        ],
        scratch_shapes=[pltpu.VMEM((2, 1536, 512), BF16)],
        compiler_params=pltpu.CompilerParams(vmem_limit_bytes=28 * MIB),
        cost_estimate=pl.CostEstimate(flops=6_500_000_000, bytes_accessed=14_000_000, transcendentals=0),
        name="build_integrals",
    )(own_f, far_f, *in_hbm(*blocks))


def ladder_kernel(t_ref, v_ref, *rest):
    start, out_ref = rest[:-1], rest[-1]
    for a in range(2):
        rows = slice(256 * a, 256 * a + 256)
        total = start[0][rows] if start else 0.0
        for d in range(4):
            total = total + dot(v_ref[d, a], t_ref[:, d].reshape(512, 512))
        if start:
            out_ref[:, a] = total.reshape(16, 16, 512).astype(BF16)
        else:
            out_ref[rows] = total


def ladder_part(*operands):
    out_shape = (16, 2, 16, 512) if len(operands) == 3 else (512, 512)
    return pl.pallas_call(
        ladder_kernel,
        out_shape=jax.ShapeDtypeStruct(out_shape, BF16 if len(operands) == 3 else F32),
        in_specs=[pl.BlockSpec(memory_space=pltpu.VMEM)] * len(operands),
        out_specs=pl.BlockSpec(memory_space=pltpu.VMEM),
        compiler_params=pltpu.CompilerParams(vmem_limit_bytes=16 * MIB),
        cost_estimate=pl.CostEstimate(flops=100_000_000_000, bytes_accessed=5_000_000, transcendentals=0),
        name="ladder_part",
    )(*in_vmem(*operands))


def sum_kernel(parts_ref, out_ref):
    total = jnp.sum(parts_ref[...].astype(F32), axis=0)
    for q in range(8):
        lanes = slice(64 * q, 64 * q + 64)
        out_ref[q % 2 * 4 + q // 2] = jnp.concatenate([total[0, :, lanes], total[1, :, lanes]], axis=-1)


def sum_parts(parts):
    return pl.pallas_call(
        sum_kernel,
        out_shape=pltpu.VMEM((8, 16, 128), F32),
        name="sum_parts",
    )(*in_vmem(parts))


def finish_kernel(parts_ref, out_ref):
    for core in range(2):
        both = jnp.sum(parts_ref[4 * core : 4 * core + 4], axis=0)
        out_ref[2 * core] = both[:, :64]
        out_ref[2 * core + 1] = both[:, 64:]


def finish(parts):
    return pl.pallas_call(
        finish_kernel,
        out_shape=jax.ShapeDtypeStruct((4, 16, 64), F32),
        name="finish",
    )(*in_vmem(parts))


def exchange(x, axis):
    return lax.all_to_all(x, axis, split_axis=0, concat_axis=0, tiled=True)


def other(x, axis):
    return lax.ppermute(x, axis, [(0, 1), (1, 0)])


def shift(x, step):
    def flat(z):
        return (z % 2) * 4 + (z // 2) % 4

    return lax.ppermute(x, RING, [(flat(z), flat((z + step) % 8)) for z in range(8)])


def per_device(window_factors, factors, amplitudes):
    window = jnp.transpose(window_factors, (0, 2, 1))
    own_w = exchange(spread(window), ("y", "x"))
    own_t = regroup(jnp.transpose(amplitudes, (1, 2, 0)))
    factors, own_w, own_t = lax.optimization_barrier((factors, own_w, own_t))
    own_f = exchange(factors.reshape(16, 64, 1536), PLANE).reshape(16, 4, 16, 1536)

    up = down = join_cores(own_w, other(own_w, "core"))
    blocks = list(up)
    for _ in range(3):
        up, down = [shift(half, 1) for half in up], [shift(half, -1) for half in down]
        blocks += up + down
    blocks += [shift(up[0], 1), shift(down[1], -1)]
    own_t, own_f, *blocks = lax.optimization_barrier((own_t, own_f, *blocks))
    amps = exchange(own_t.reshape(32, 64, 512), ROW).reshape(32, 4, 16, 512)
    own_v, far_v = build_integrals(own_f, other(own_f, "core"), blocks)
    part = ladder_part(amps, own_v)
    part = ladder_part(other(amps, "core"), far_v, part)

    part = sum_parts(exchange(part, PLANE))
    return jnp.transpose(finish(exchange(part, ("core", "zh"))), (2, 0, 1))


def solution(mesh):
    fine = Mesh(mesh.devices.reshape(4, 2, 4, 4, 2), ("y", "zl", "x", "zh", "core"))
    row, col = ROW, ("zh", "core")
    return jax.shard_map(
        per_device,
        mesh=fine,
        in_specs=(P(None, col, row), P(col, row, None), P(None, row, col)),
        out_specs=P(col, None, row),
        check_vma=False,
    )
```

```python
import jax
import jax.numpy as jnp
from jax import lax
from jax.experimental import pallas as pl
from jax.experimental.pallas import tpu as pltpu
from jax.sharding import Mesh
from jax.sharding import PartitionSpec as P

BF16 = jnp.bfloat16
F32 = jnp.float32
PLANE = ("x", "y")
ROW = ("y", "zl", "x")
RING = ("zl", "zh")
MIB = 1024 * 1024


def in_vmem(*arrays):
    return [pltpu.with_memory_space_constraint(a, pltpu.VMEM) for a in arrays]


def in_hbm(*arrays):
    return [pltpu.with_memory_space_constraint(a, pltpu.HBM) for a in arrays]


def dot(left, right):
    return lax.dot_general(left, right, (((1,), (0,)), ((), ())), preferred_element_type=F32)


def spread_kernel(w_ref, out_ref):
    for half in range(2):
        block = jnp.concatenate([w_ref[2 * half], w_ref[2 * half + 1]], axis=-1)
        for s in range(16):
            out_ref[s, half] = block


def spread(window):
    return pl.pallas_call(
        spread_kernel,
        out_shape=pltpu.VMEM((16, 2, 48, 128), BF16),
        name="spread_window",
    )(*in_vmem(window))


def join_kernel(own_ref, far_ref, *out_refs):
    core = lax.axis_index("core")
    mine, theirs = own_ref[:, core], far_ref[:, core]
    first = jnp.where(core == 0, mine, theirs)
    second = jnp.where(core == 0, theirs, mine)
    for a in range(2):
        lanes = slice(64 * a, 64 * a + 64)
        block = jnp.concatenate([first[..., lanes], second[..., lanes]], axis=-1)
        out_refs[0][:, a] = block[:8]
        out_refs[1][:, a] = block[8:]


def join_cores(own, far):
    return pl.pallas_call(
        join_kernel,
        out_shape=[pltpu.VMEM((8, 2, 48, 128), BF16)] * 2,
        name="join_window",
    )(*in_vmem(own, far))


def regroup_kernel(t_ref, out_ref):
    dest = lax.broadcasted_iota(jnp.int32, (256, 256), 0)
    src = lax.broadcasted_iota(jnp.int32, (256, 256), 1)
    select = jnp.where(src == (dest % 16) * 16 + dest // 16, 1.0, 0.0).astype(BF16)
    rows = dot(select, t_ref[...].reshape(256, 512)).astype(BF16).reshape(4, 4, 16, 512)
    out_ref[:, 0, 0] = rows
    out_ref[:, 1, 0] = rows


def regroup(amps):
    return pl.pallas_call(
        regroup_kernel,
        out_shape=jax.ShapeDtypeStruct((4, 2, 4, 4, 16, 512), BF16),
        grid=(4,),
        in_specs=[pl.BlockSpec((16, 16, 512), lambda g: (0, g, 0))],
        out_specs=pl.BlockSpec((4, 2, 1, 4, 16, 512), lambda g: (0, 0, g, 0, 0, 0)),
        name="regroup_amplitudes",
    )(amps).reshape(32, 4, 16, 512)


def integrals_kernel(own_f, far_f, *rest):
    blocks, (own_v, far_v, window) = rest[:-3], rest[-3:]
    g = pl.program_id(0)

    @pl.when(g == 0)
    def _():
        z = 2 * lax.axis_index("zh") + lax.axis_index("zl")
        for n, ref in enumerate(blocks):
            at = (z + (0, -1, 1, -2, 2, -3, 3, 4)[n // 2] + 8) % 8
            row, lane = (at % 2) * 192, pl.multiple_of((at // 2) * 128, 128)
            for y in range(2):
                rows = pl.ds(pl.multiple_of((y + n % 2 * 2) * 384 + row, 192), 192)
                for a in range(2):
                    window[a, rows, pl.ds(lane, 128)] = ref[4 * y : 4 * y + 4, a].reshape(192, 128)

    def step(f_ref, out_ref):
        factors = f_ref[...].reshape(512, 1536)
        for a in range(2):
            integrals = dot(factors, window[a]).astype(BF16).reshape(16, 2, 16, 512)
            for d in range(2):
                out_ref[d, a] = integrals[:, d].reshape(256, 512)

    @pl.when(g < 2)
    def _():
        step(own_f, own_v)

    @pl.when(g >= 2)
    def _():
        step(far_f, far_v)


def build_integrals(own_f, far_f, blocks):
    return pl.pallas_call(
        integrals_kernel,
        out_shape=[pltpu.VMEM((4, 2, 256, 512), BF16)] * 2,
        grid=(4,),
        in_specs=[
            pl.BlockSpec((16, 2, 16, 1536), lambda g: (0, jnp.minimum(g, 1), 0, 0)),
            pl.BlockSpec((16, 2, 16, 1536), lambda g: (0, jnp.maximum(g - 2, 0), 0, 0)),
        ]
        + [pl.BlockSpec(b.shape, lambda g: (0, 0, 0, 0)) for b in blocks],
        out_specs=[
            pl.BlockSpec((2, 2, 256, 512), lambda g: (jnp.minimum(g, 1), 0, 0, 0)),
            pl.BlockSpec((2, 2, 256, 512), lambda g: (jnp.maximum(g - 2, 0), 0, 0, 0)),
        ],
        scratch_shapes=[pltpu.VMEM((2, 1536, 512), BF16)],
        compiler_params=pltpu.CompilerParams(vmem_limit_bytes=28 * MIB),
        cost_estimate=pl.CostEstimate(flops=6_500_000_000, bytes_accessed=14_000_000, transcendentals=0),
        name="build_integrals",
    )(own_f, far_f, *in_hbm(*blocks))


def ladder_kernel(t_ref, v_ref, *rest):
    start, out_ref = rest[:-1], rest[-1]
    for a in range(2):
        rows = slice(256 * a, 256 * a + 256)
        total = start[0][rows] if start else 0.0
        for d in range(4):
            total = total + dot(v_ref[d, a], t_ref[:, d].reshape(512, 512))
        if start:
            out_ref[:, a] = total.reshape(16, 16, 512).astype(BF16)
        else:
            out_ref[rows] = total


def ladder_part(*operands):
    out_shape = (16, 2, 16, 512) if len(operands) == 3 else (512, 512)
    return pl.pallas_call(
        ladder_kernel,
        out_shape=jax.ShapeDtypeStruct(out_shape, BF16 if len(operands) == 3 else F32),
        in_specs=[pl.BlockSpec(memory_space=pltpu.VMEM)] * len(operands),
        out_specs=pl.BlockSpec(memory_space=pltpu.VMEM),
        compiler_params=pltpu.CompilerParams(vmem_limit_bytes=16 * MIB),
        cost_estimate=pl.CostEstimate(flops=100_000_000_000, bytes_accessed=5_000_000, transcendentals=0),
        name="ladder_part",
    )(*in_vmem(*operands))


def sum_kernel(parts_ref, out_ref):
    total = jnp.sum(parts_ref[...].astype(F32), axis=0)
    for q in range(8):
        lanes = slice(64 * q, 64 * q + 64)
        out_ref[q % 2 * 4 + q // 2] = jnp.concatenate([total[0, :, lanes], total[1, :, lanes]], axis=-1)


def sum_parts(parts):
    return pl.pallas_call(
        sum_kernel,
        out_shape=pltpu.VMEM((8, 16, 128), F32),
        name="sum_parts",
    )(*in_vmem(parts))


def finish_kernel(parts_ref, out_ref):
    for core in range(2):
        both = jnp.sum(parts_ref[4 * core : 4 * core + 4], axis=0)
        out_ref[2 * core] = both[:, :64]
        out_ref[2 * core + 1] = both[:, 64:]


def finish(parts):
    return pl.pallas_call(
        finish_kernel,
        out_shape=jax.ShapeDtypeStruct((4, 16, 64), F32),
        name="finish",
    )(*in_vmem(parts))


def exchange(x, axis):
    return lax.all_to_all(x, axis, split_axis=0, concat_axis=0, tiled=True)


def other(x, axis):
    return lax.ppermute(x, axis, [(0, 1), (1, 0)])


def shift(x, step):
    def flat(z):
        return (z % 2) * 4 + (z // 2) % 4

    return lax.ppermute(x, RING, [(flat(z), flat((z + step) % 8)) for z in range(8)])


def per_device(window_factors, factors, amplitudes):
    window = jnp.transpose(window_factors, (0, 2, 1))
    own_w = exchange(spread(window), ("y", "x"))
    factors, own_w, amplitudes = lax.optimization_barrier((factors, own_w, amplitudes))
    own_t = regroup(jnp.transpose(amplitudes, (1, 2, 0)))
    own_f = exchange(factors.reshape(16, 64, 1536), PLANE).reshape(16, 4, 16, 1536)

    up = down = join_cores(own_w, other(own_w, "core"))
    blocks = list(up)
    for _ in range(3):
        up, down = [shift(half, 1) for half in up], [shift(half, -1) for half in down]
        blocks += up + down
    blocks += [shift(up[0], 1), shift(down[1], -1)]
    own_t, own_f, *blocks = lax.optimization_barrier((own_t, own_f, *blocks))
    amps = exchange(own_t.reshape(32, 64, 512), ROW).reshape(32, 4, 16, 512)
    own_v, far_v = build_integrals(own_f, other(own_f, "core"), blocks)
    part = ladder_part(amps, own_v)
    part = ladder_part(other(amps, "core"), far_v, part)

    part = sum_parts(exchange(part, PLANE))
    return jnp.transpose(finish(exchange(part, ("core", "zh"))), (2, 0, 1))


def solution(mesh):
    fine = Mesh(mesh.devices.reshape(4, 2, 4, 4, 2), ("y", "zl", "x", "zh", "core"))
    row, col = ROW, ("zh", "core")
    return jax.shard_map(
        per_device,
        mesh=fine,
        in_specs=(P(None, col, row), P(col, row, None), P(None, row, col)),
        out_specs=P(col, None, row),
        check_vma=False,
    )
```

```python
import jax
import jax.numpy as jnp
from jax import lax
from jax.experimental import pallas as pl
from jax.experimental.pallas import tpu as pltpu
from jax.sharding import Mesh
from jax.sharding import PartitionSpec as P

BF16 = jnp.bfloat16
F32 = jnp.float32
PLANE = ("x", "y")
ROW = ("y", "zl", "x")
RING = ("zl", "zh")
MIB = 1024 * 1024


def in_vmem(*arrays):
    return [pltpu.with_memory_space_constraint(a, pltpu.VMEM) for a in arrays]


def in_hbm(*arrays):
    return [pltpu.with_memory_space_constraint(a, pltpu.HBM) for a in arrays]


def dot(left, right):
    return lax.dot_general(left, right, (((1,), (0,)), ((), ())), preferred_element_type=F32)


def spread_kernel(w_ref, out_ref):
    for half in range(2):
        block = jnp.concatenate([w_ref[2 * half], w_ref[2 * half + 1]], axis=-1)
        for s in range(16):
            out_ref[s, half] = block


def spread(window):
    return pl.pallas_call(
        spread_kernel,
        out_shape=pltpu.VMEM((16, 2, 48, 128), BF16),
        name="spread_window",
    )(*in_vmem(window))


def join_kernel(own_ref, far_ref, *out_refs):
    core = lax.axis_index("core")
    mine, theirs = own_ref[:, core], far_ref[:, core]
    first = jnp.where(core == 0, mine, theirs)
    second = jnp.where(core == 0, theirs, mine)
    for a in range(2):
        lanes = slice(64 * a, 64 * a + 64)
        block = jnp.concatenate([first[..., lanes], second[..., lanes]], axis=-1)
        out_refs[0][:, a] = block[:8]
        out_refs[1][:, a] = block[8:]


def join_cores(own, far):
    return pl.pallas_call(
        join_kernel,
        out_shape=[pltpu.VMEM((8, 2, 48, 128), BF16)] * 2,
        name="join_window",
    )(*in_vmem(own, far))


def regroup_kernel(t_ref, out_ref):
    dest = lax.broadcasted_iota(jnp.int32, (256, 256), 0)
    src = lax.broadcasted_iota(jnp.int32, (256, 256), 1)
    select = jnp.where(src == (dest % 16) * 16 + dest // 16, 1.0, 0.0).astype(BF16)
    rows = dot(select, t_ref[...].reshape(256, 512)).astype(BF16).reshape(4, 4, 16, 512)
    out_ref[:, 0, 0] = rows
    out_ref[:, 1, 0] = rows


def regroup(amps):
    return pl.pallas_call(
        regroup_kernel,
        out_shape=jax.ShapeDtypeStruct((4, 2, 4, 4, 16, 512), BF16),
        grid=(4,),
        in_specs=[pl.BlockSpec((16, 16, 512), lambda g: (0, g, 0))],
        out_specs=pl.BlockSpec((4, 2, 1, 4, 16, 512), lambda g: (0, 0, g, 0, 0, 0)),
        name="regroup_amplitudes",
    )(amps).reshape(32, 4, 16, 512)


def integrals_kernel(own_f, far_f, *rest):
    blocks, (own_v, far_v, window) = rest[:-3], rest[-3:]
    g = pl.program_id(0)

    @pl.when(g == 0)
    def _():
        z = 2 * lax.axis_index("zh") + lax.axis_index("zl")
        for n, ref in enumerate(blocks):
            at = (z + (0, -1, 1, -2, 2, -3, 3, 4)[n // 2] + 8) % 8
            row, lane = (at % 2) * 192, pl.multiple_of((at // 2) * 128, 128)
            for y in range(2):
                rows = pl.ds(pl.multiple_of((y + n % 2 * 2) * 384 + row, 192), 192)
                for a in range(2):
                    window[a, rows, pl.ds(lane, 128)] = ref[4 * y : 4 * y + 4, a].reshape(192, 128)

    def step(f_ref, out_ref):
        factors = f_ref[...].reshape(512, 1536)
        for a in range(2):
            integrals = dot(factors, window[a]).astype(BF16).reshape(16, 2, 16, 512)
            for d in range(2):
                out_ref[d, a] = integrals[:, d].reshape(256, 512)

    @pl.when(g < 2)
    def _():
        step(own_f, own_v)

    @pl.when(g >= 2)
    def _():
        step(far_f, far_v)


def build_integrals(own_f, far_f, blocks):
    return pl.pallas_call(
        integrals_kernel,
        out_shape=[pltpu.HBM((4, 2, 256, 512), BF16)] * 2,
        grid=(4,),
        in_specs=[
            pl.BlockSpec((16, 2, 16, 1536), lambda g: (0, jnp.minimum(g, 1), 0, 0)),
            pl.BlockSpec((16, 2, 16, 1536), lambda g: (0, jnp.maximum(g - 2, 0), 0, 0)),
        ]
        + [pl.BlockSpec(b.shape, lambda g: (0, 0, 0, 0)) for b in blocks],
        out_specs=[
            pl.BlockSpec((2, 2, 256, 512), lambda g: (jnp.minimum(g, 1), 0, 0, 0)),
            pl.BlockSpec((2, 2, 256, 512), lambda g: (jnp.maximum(g - 2, 0), 0, 0, 0)),
        ],
        scratch_shapes=[pltpu.VMEM((2, 1536, 512), BF16)],
        compiler_params=pltpu.CompilerParams(vmem_limit_bytes=28 * MIB),
        cost_estimate=pl.CostEstimate(flops=6_500_000_000, bytes_accessed=14_000_000, transcendentals=0),
        name="build_integrals",
    )(own_f, far_f, *in_hbm(*blocks))


def ladder_kernel(t_ref, v_ref, *rest):
    start, out_ref = rest[:-1], rest[-1]
    for a in range(2):
        rows = slice(256 * a, 256 * a + 256)
        total = start[0][rows] if start else 0.0
        for d in range(4):
            total = total + dot(v_ref[d, a], t_ref[:, d].reshape(512, 512))
        if start:
            out_ref[:, a] = total.reshape(16, 16, 512).astype(BF16)
        else:
            out_ref[rows] = total


def ladder_part(*operands):
    out_shape = (16, 2, 16, 512) if len(operands) == 3 else (512, 512)
    return pl.pallas_call(
        ladder_kernel,
        out_shape=jax.ShapeDtypeStruct(out_shape, BF16 if len(operands) == 3 else F32),
        in_specs=[pl.BlockSpec(memory_space=pltpu.VMEM)] * len(operands),
        out_specs=pl.BlockSpec(memory_space=pltpu.VMEM),
        compiler_params=pltpu.CompilerParams(vmem_limit_bytes=16 * MIB),
        cost_estimate=pl.CostEstimate(flops=100_000_000_000, bytes_accessed=5_000_000, transcendentals=0),
        name="ladder_part",
    )(*in_vmem(*operands))


def sum_kernel(parts_ref, out_ref):
    total = jnp.sum(parts_ref[...].astype(F32), axis=0)
    for q in range(8):
        lanes = slice(64 * q, 64 * q + 64)
        out_ref[q % 2 * 4 + q // 2] = jnp.concatenate([total[0, :, lanes], total[1, :, lanes]], axis=-1)


def sum_parts(parts):
    return pl.pallas_call(
        sum_kernel,
        out_shape=pltpu.VMEM((8, 16, 128), F32),
        name="sum_parts",
    )(*in_vmem(parts))


def finish_kernel(parts_ref, out_ref):
    for core in range(2):
        both = jnp.sum(parts_ref[4 * core : 4 * core + 4], axis=0)
        out_ref[2 * core] = both[:, :64]
        out_ref[2 * core + 1] = both[:, 64:]


def finish(parts):
    return pl.pallas_call(
        finish_kernel,
        out_shape=jax.ShapeDtypeStruct((4, 16, 64), F32),
        name="finish",
    )(*in_vmem(parts))


def exchange(x, axis):
    return lax.all_to_all(x, axis, split_axis=0, concat_axis=0, tiled=True)


def other(x, axis):
    return lax.ppermute(x, axis, [(0, 1), (1, 0)])


def shift(x, step):
    def flat(z):
        return (z % 2) * 4 + (z // 2) % 4

    return lax.ppermute(x, RING, [(flat(z), flat((z + step) % 8)) for z in range(8)])


def per_device(window_factors, factors, amplitudes):
    window = jnp.transpose(window_factors, (0, 2, 1))
    own_w = exchange(spread(window), ("y", "x"))
    factors, own_w, amplitudes = lax.optimization_barrier((factors, own_w, amplitudes))
    own_t = regroup(jnp.transpose(amplitudes, (1, 2, 0)))
    own_f = exchange(factors.reshape(16, 64, 1536), PLANE).reshape(16, 4, 16, 1536)

    up = down = join_cores(own_w, other(own_w, "core"))
    blocks = list(up)
    for _ in range(3):
        up, down = [shift(half, 1) for half in up], [shift(half, -1) for half in down]
        blocks += up + down
    blocks += [shift(up[0], 1), shift(down[1], -1)]
    own_t, own_f, *blocks = lax.optimization_barrier((own_t, own_f, *blocks))
    amps = exchange(own_t.reshape(32, 64, 512), ROW).reshape(32, 4, 16, 512)
    own_v, far_v = build_integrals(own_f, other(own_f, "core"), blocks)
    part = ladder_part(amps, own_v)
    part = ladder_part(other(amps, "core"), far_v, part)

    part = sum_parts(exchange(part, PLANE))
    return jnp.transpose(finish(exchange(part, ("core", "zh"))), (2, 0, 1))


def solution(mesh):
    fine = Mesh(mesh.devices.reshape(4, 2, 4, 4, 2), ("y", "zl", "x", "zh", "core"))
    row, col = ROW, ("zh", "core")
    return jax.shard_map(
        per_device,
        mesh=fine,
        in_specs=(P(None, col, row), P(col, row, None), P(None, row, col)),
        out_specs=P(col, None, row),
        check_vma=False,
    )
```
